512 devices in a mesh: dp: 32 (over x_hi, y, core), mp: 16 (over x_lo, z).
Axes of the slice: x: 4 (x_hi: 2, x_lo: 2; x = x_hi * 2 + x_lo), y: 8, z: 8, core: 2. Of those that a mesh axis runs over, the one named last changes fastest.
Arguments:
- tokens: bfloat16 [8192, 6144], P('dp', 'mp'), may hold values from -200 to 200
- ln_gain: bfloat16 [6144], P('mp'), may hold values from 0.2 to 2.8
- qkv_weight: bfloat16 [3, 6144, 4096], P(None, 'dp', 'mp'), may hold values from -0.08292543 to 0.08292543
- qk_gain: float32 [2, 128], replicated, may hold values from 0.5 to 2
- cotangent: bfloat16 [8192, 4096], P('dp', 'mp'), may hold values from -6 to 6
Outputs:
- attended: bfloat16 [8192, 4096], P('dp', 'mp')
- grad_tokens: bfloat16 [8192, 6144], P('dp', 'mp')
The draws below stay inside these ranges and needn't reach their ends.
All inputs are finite; a program needn't handle non-finite values.
Results may differ from the reference program's by a relative error of at most 0.034.
Values may be sent and summed in bfloat16 or wider, within the bound.
No kernel may reach another device: no remote copies, remote signals or barrier semaphores. Data moves between devices by JAX's collectives and lax.ppermute only.
A program may use at most 64 MiB of HBM per device.

```python
import math
import jax
import jax.numpy as jnp
from jax import lax

D = 6144
HEADSZ = 128
PATCH = 256
HEADS = 32
HD = 4096
TOKENS = 8192
N_MP = 16


def draw_tokens(key, part):
    key = jax.random.fold_in(key, 11)
    keys_all = jax.random.split(key, 4)
    base = jnp.clip(jax.random.normal(keys_all[0], (TOKENS, D), jnp.float32), -4.0, 4.0)
    row_scale = jnp.exp(jax.random.uniform(keys_all[1], (TOKENS, 1), jnp.float32, 0.0, math.log(10.0)))
    col_scale = jnp.exp(jax.random.uniform(keys_all[2], (1, D), jnp.float32, math.log(0.5), math.log(2.0)))
    offsets = jax.random.uniform(keys_all[3], (1, D), jnp.float32, -1.0, 1.0)
    return (row_scale * col_scale * (base + offsets)).astype(jnp.bfloat16)


def draw_ln_gain(key, part):
    key = jax.random.fold_in(key, 12)
    ramp = jnp.arange(D, dtype=jnp.float32) / D
    factor = jax.random.uniform(key, (D,), jnp.float32, 0.7, 1.3)
    result = (0.5 + ramp) * factor
    return result.astype(jnp.bfloat16)


def draw_qkv_weight(key, part):
    key = jax.random.fold_in(key, 13)
    first, second = jax.random.split(key, 2)
    common = jnp.clip(jax.random.normal(second, (3, 1, HD), jnp.float32), -3.0, 3.0)
    base = jnp.clip(jax.random.normal(first, (3, D, HD), jnp.float32), -4.0, 4.0)
    result = (base + 0.8 * common) * D ** (-0.5)
    return result.astype(jnp.bfloat16)


def block_scale(stream_key, shape, pieces, low, high):
    loudness, own = 1.0, jax.random.fold_in(stream_key, 6)
    for axis_at, shards_of in pieces:
        heights = jnp.exp(jax.random.uniform(jax.random.fold_in(own, axis_at), (shards_of,), jnp.float32, low / len(pieces), high / len(pieces)))
        loudness = loudness * jnp.repeat(heights, shape[axis_at] // shards_of).reshape([-1 if axis == axis_at else 1 for axis in range(len(shape))])
    return loudness


def noise(rng, extent, scale, reach, cuts=(), kind=jnp.bfloat16):
    drawn = scale * jax.random.normal(rng, extent, jnp.float32)
    if cuts:
        drawn = drawn * block_scale(rng, extent, cuts, -0.22, 0.18)
    return jnp.clip(drawn, -reach, reach).astype(kind)


def setup_inputs(seed: int = 0) -> dict:
    streams_of = jax.random.split(jax.random.key(seed), 6)
    return {
        "tokens": draw_tokens(jax.random.fold_in(streams_of[5], 71), 0),
        "ln_gain": draw_ln_gain(jax.random.fold_in(streams_of[5], 71), 0),
        "qkv_weight": draw_qkv_weight(jax.random.fold_in(streams_of[5], 71), 0),
        "qk_gain": jnp.clip(jax.random.uniform(streams_of[3], (2, HEADSZ), jnp.float32, 0.5, 2.0), 0.5, 2.0),
        "cotangent": noise(streams_of[4], (TOKENS, HD), 1.0, 6.0, ((0, 32), (1, 16))),
    }


def norm_rows(field):
    row_mean = lax.optimization_barrier(jnp.mean(field, axis=-1, keepdims=True))
    centred = field - row_mean
    inv_std = lax.rsqrt(lax.optimization_barrier(jnp.mean(centred * centred, axis=-1, keepdims=True)) + 1e-06)
    return (centred * inv_std, inv_std)

def norm_back(grad_hat, x_hat, inv_std):
    first = lax.optimization_barrier(jnp.mean(grad_hat, axis=-1, keepdims=True))
    second = lax.optimization_barrier(jnp.mean(grad_hat * x_hat, axis=-1, keepdims=True))
    return inv_std * (grad_hat - first - x_hat * second)

def reference(tokens, ln_gain, qkv_weight, qk_gain, cotangent):
    f32 = jnp.float32
    bf16 = jnp.bfloat16
    images = TOKENS // PATCH
    x_hat, inv_std = norm_rows(tokens.astype(f32))
    normed = (x_hat * ln_gain.astype(f32)).astype(bf16)
    weight_f = qkv_weight.astype(f32)
    projected = jnp.einsum('td,idf->itf', normed.astype(f32), weight_f)
    split = projected.reshape(3, images, PATCH, HEADS, HEADSZ)
    q_hat, q_inv = norm_rows(split[0])
    k_hat, k_inv = norm_rows(split[1])
    queries = (q_hat * qk_gain[0]).astype(bf16).astype(f32)
    keys_n = (k_hat * qk_gain[1]).astype(bf16).astype(f32)
    values = split[2].astype(bf16).astype(f32)
    scale = HEADSZ ** (-0.5)
    scores = jnp.einsum('bqhe,bkhe->bhqk', queries, keys_n) * scale
    expo = jnp.exp(scores)
    probs = expo / lax.optimization_barrier(jnp.sum(expo, axis=-1, keepdims=True))
    weights_b = probs.astype(bf16).astype(f32)
    attended = jnp.einsum('bhqk,bkhe->bqhe', weights_b, values).astype(bf16).reshape(TOKENS, HD)
    upstream = cotangent.astype(f32).reshape(images, PATCH, HEADS, HEADSZ)
    d_probs = jnp.einsum('bqhe,bkhe->bhqk', upstream, values)
    d_values = jnp.einsum('bhqk,bqhe->bkhe', weights_b, upstream).astype(bf16)
    inner = lax.optimization_barrier(jnp.sum(probs * d_probs, axis=-1, keepdims=True))
    d_scores = (probs * (d_probs - inner) * scale).astype(bf16).astype(f32)
    d_queries = jnp.einsum('bhqk,bkhe->bqhe', d_scores, keys_n)
    d_keys = jnp.einsum('bhqk,bqhe->bkhe', d_scores, queries)
    grad_q = norm_back(d_queries * qk_gain[0], q_hat, q_inv).astype(bf16)
    grad_k = norm_back(d_keys * qk_gain[1], k_hat, k_inv).astype(bf16)
    grads = jnp.stack([grad_q, grad_k, d_values]).reshape(3, TOKENS, HD).astype(f32)
    group = HD // N_MP
    d_normed = jnp.zeros((TOKENS, D), f32)
    for shard in range(N_MP):
        lower = shard * group
        partial_sum = jnp.einsum('itf,idf->td', grads[:, :, lower:lower + group], weight_f[:, :, lower:lower + group])
        rounded = lax.optimization_barrier(partial_sum.astype(bf16))
        d_normed = d_normed + rounded.astype(f32)
    grad_tokens = norm_back(d_normed * ln_gain.astype(f32), x_hat, inv_std).astype(bf16)
    return (attended, grad_tokens)
```

```python
import jax
import jax.numpy as jnp
from jax import lax
from jax.experimental import pallas as pl
from jax.experimental.pallas import tpu as pltpu
from jax.sharding import Mesh, PartitionSpec as P

HEADSZ = 128
PATCH = 256
EPS = 1e-06
GAIN_ROWS = 16
F32 = jnp.float32
BF16 = jnp.bfloat16
VMEM = pl.BlockSpec(memory_space=pltpu.VMEM)
SMEM = pl.BlockSpec(memory_space=pltpu.SMEM)


def params(mib):
    return pltpu.CompilerParams(vmem_limit_bytes=mib * 1024 * 1024)


def dot(a, b, ca, cb):
    return lax.dot_general(a, b, (((ca,), (cb,)), ((), ())), preferred_element_type=F32)


def lane_fold(x):
    total = x[:, :128]
    for at in range(128, x.shape[1], 128):
        total = total + x[:, at : at + 128]
    return total


def normalise_kernel(feat_all, z_ref, *refs):
    pieces = refs[:-2]
    normed_ref, stat_ref = refs[-2:]
    z = z_ref[0]
    zs = 8
    blocks = []
    own = pieces[0]
    for xl in range(2):
        blocks.append((own, xl, xl * zs + z))
    for step in range(1, 4):
        for xl in range(2):
            blocks.append((pieces[2 * step - 1], xl, xl * zs + lax.rem(z + zs - step, zs)))
            blocks.append((pieces[2 * step], xl, xl * zs + lax.rem(z + step, zs)))
    far = lax.rem(z + 4, zs)
    blocks.append((pieces[7], 0, far))
    blocks.append((pieces[8], 0, zs + far))
    rows = PATCH
    total = jnp.zeros((rows, 128), F32)
    for ref, at, _ in blocks:
        total = total + lane_fold(ref[at, :rows, :].astype(F32))
    mean = jnp.sum(total, axis=1, keepdims=True) / feat_all
    total = jnp.zeros((rows, 128), F32)
    for ref, at, _ in blocks:
        centred = ref[at, :rows, :].astype(F32) - mean
        total = total + lane_fold(centred * centred)
    inv = lax.rsqrt(jnp.sum(total, axis=1, keepdims=True) / feat_all + EPS)
    for ref, at, place in blocks:
        x_hat = (ref[at, :rows, :].astype(F32) - mean) * inv
        gain = ref[at, rows : rows + 1, :].astype(F32)
        normed_ref[place, :rows, :] = (x_hat * gain).astype(BF16)
        normed_ref[place, rows:, :] = ref[at, rows:, :]
    stat_ref[0] = jnp.broadcast_to(mean, (rows, 128))
    stat_ref[1] = jnp.broadcast_to(inv, (rows, 128))


def norm128(x):
    mean = jnp.mean(x, axis=1, keepdims=True)
    centred = x - mean
    inv = lax.rsqrt(jnp.mean(centred * centred, axis=1, keepdims=True) + EPS)
    return centred * inv, inv


def norm128_back(grad_hat, x_hat, inv):
    first = jnp.mean(grad_hat, axis=1, keepdims=True)
    second = jnp.mean(grad_hat * x_hat, axis=1, keepdims=True)
    return inv * (grad_hat - first - x_hat * second)


def attention_kernel(normed_ref, w_ref, qk_ref, cot_ref, out_ref, grads_ref, stat_ref, acc):
    n_m = normed_ref.shape[0]
    third = w_ref.shape[2] // 3
    width = w_ref.shape[3]
    heads = width // HEADSZ
    acc[...] = jnp.zeros_like(acc)

    def step(m, carry):
        xh = m // 8
        y = lax.rem(m, 8)
        x = normed_ref[m]
        for i in range(3):
            w = jnp.concatenate(
                [w_ref[2 * y + c, xh, i * third : (i + 1) * third, :] for c in range(2)], axis=0
            )
            acc[:, i * width : (i + 1) * width] += dot(x, w, 1, 0)
        return carry

    lax.fori_loop(0, n_m, step, 0)
    rows = PATCH
    scale = HEADSZ ** (-0.5)
    gain_q = qk_ref[0:1, :]
    gain_k = qk_ref[1:2, :]
    first = jnp.zeros((rows, 128), F32)
    second = jnp.zeros((rows, 128), F32)
    for h in range(heads):
        cols = [slice(i * width + h * HEADSZ, i * width + (h + 1) * HEADSZ) for i in range(3)]
        own = slice(h * HEADSZ, (h + 1) * HEADSZ)
        proj = [acc[:rows, c] for c in cols]
        q_hat, q_inv = norm128(proj[0])
        k_hat, k_inv = norm128(proj[1])
        queries = (q_hat * gain_q).astype(BF16)
        keys = (k_hat * gain_k).astype(BF16)
        values = proj[2].astype(BF16)
        expo = jnp.exp(dot(queries, keys, 1, 1) * scale)
        probs = expo / jnp.sum(expo, axis=1, keepdims=True)
        weights_b = probs.astype(BF16)
        out_ref[:, own] = dot(weights_b, values, 1, 0).astype(BF16)
        upstream = cot_ref[:, own]
        d_probs = dot(upstream, values, 1, 1)
        d_values = dot(weights_b, upstream, 0, 0).astype(BF16)
        inner = jnp.sum(probs * d_probs, axis=1, keepdims=True)
        d_scores = (probs * (d_probs - inner) * scale).astype(BF16)
        d_queries = dot(d_scores, keys, 1, 0)
        d_keys = dot(d_scores, queries, 0, 0)
        grad_q = norm128_back(d_queries * gain_q, q_hat, q_inv).astype(BF16)
        grad_k = norm128_back(d_keys * gain_k, k_hat, k_inv).astype(BF16)
        for i, grad in enumerate((grad_q, grad_k, d_values)):
            grads_ref[i, :, own] = grad
            wide = grad.astype(F32)
            first = first + wide * acc[rows : rows + 1, cols[i]]
            second = second + wide * proj[i]
    stat_ref[0:1, :] = jnp.sum(first, axis=1)[None, :]
    stat_ref[1:2, :] = jnp.sum(second, axis=1)[None, :]


def backward_kernel(grads_ref, w_ref, out_ref):
    third = w_ref.shape[2] // 3

    def step(m, carry):
        xh = m // 8
        y = lax.rem(m, 8)
        total = None
        for i in range(3):
            w = jnp.concatenate(
                [w_ref[2 * y + c, xh, i * third : (i + 1) * third, :] for c in range(2)], axis=0
            )
            term = dot(grads_ref[i], w, 1, 1)
            total = term if total is None else total + term
        out_ref[2 * y + xh] = total.astype(BF16)
        return carry

    lax.fori_loop(0, out_ref.shape[0], step, 0)


def final_kernel(feat_all, mine_ref, other_ref, tok_ref, gain_ref, stat_ref, sums_ref, out_ref):
    b = (mine_ref[...].astype(F32) + other_ref[...].astype(F32)) * gain_ref[0:1, :].astype(F32)
    mean = stat_ref[0, :, 0:1]
    inv = stat_ref[1, :, 0:1]
    x_hat = (tok_ref[...].astype(F32) - mean) * inv
    first = sums_ref[:, 0:1] / feat_all
    second = sums_ref[:, 1:2] / feat_all
    out_ref[...] = (inv * (b - first - x_hat * second)).astype(BF16)


def ring(n, step):
    return [(i, (i + step) % n) for i in range(n)]


def per_device(tokens, ln_gain, qkv_weight, qk_gain, cotangent):
    rows, feat = tokens.shape
    width = qkv_weight.shape[2]
    feat_all = feat * 16
    z = lax.axis_index("z").astype(jnp.int32)

    weights = qkv_weight.reshape(-1, width)
    weights = lax.all_gather(weights, "xh", axis=0)
    weights = lax.all_gather(weights, ("y", "c"), axis=0)

    gain = jnp.broadcast_to(ln_gain[None, :], (GAIN_ROWS, feat))
    own = lax.all_gather(jnp.concatenate([tokens, gain], axis=0), "xl", axis=0)
    pieces = [own]
    ahead = behind = own
    for _ in range(3):
        ahead = lax.ppermute(ahead, "z", ring(8, 1))
        behind = lax.ppermute(behind, "z", ring(8, -1))
        pieces += [ahead, behind]
    pieces.append(lax.ppermute(ahead[:1], "z", ring(8, 1)))
    pieces.append(lax.ppermute(behind[1:], "z", ring(8, -1)))

    normed, stats = pl.pallas_call(
        lambda *refs: normalise_kernel(feat_all, *refs),
        out_shape=(
            jax.ShapeDtypeStruct((16, rows + GAIN_ROWS, feat), BF16),
            jax.ShapeDtypeStruct((2, rows, 128), F32),
        ),
        in_specs=[SMEM] + [VMEM] * len(pieces),
        out_specs=(VMEM, VMEM),
        compiler_params=params(32),
        name="normalise",
    )(z[None], *pieces)

    attended, grads, sums = pl.pallas_call(
        attention_kernel,
        out_shape=(
            jax.ShapeDtypeStruct((rows, width), BF16),
            jax.ShapeDtypeStruct((3, rows, width), BF16),
            jax.ShapeDtypeStruct((2, rows), F32),
        ),
        in_specs=[VMEM] * 4,
        out_specs=(VMEM,) * 3,
        scratch_shapes=[pltpu.VMEM((rows + GAIN_ROWS, 3 * width), F32)],
        compiler_params=params(40),
        name="attention",
    )(normed, weights, qk_gain, cotangent)

    partial = pl.pallas_call(
        backward_kernel,
        out_shape=jax.ShapeDtypeStruct((16, rows, feat), BF16),
        in_specs=[VMEM] * 2,
        out_specs=VMEM,
        compiler_params=params(40),
        name="backward",
    )(grads, weights)

    sums = lax.psum(sums, ("xl", "z"))
    reduced = lax.psum_scatter(partial.reshape(8, 2, rows, feat), "z", scatter_dimension=0, tiled=True)
    xl = lax.axis_index("xl")
    mine = lax.dynamic_index_in_dim(reduced[0], xl, 0, keepdims=False)
    other = lax.dynamic_index_in_dim(reduced[0], 1 - xl, 0, keepdims=False)
    other = lax.ppermute(other, "xl", ring(2, 1))
    grad_tokens = pl.pallas_call(
        lambda *refs: final_kernel(feat_all, *refs),
        out_shape=jax.ShapeDtypeStruct((rows, feat), BF16),
        in_specs=[VMEM] * 6,
        out_specs=VMEM,
        name="final_norm",
    )(mine, other, tokens, gain, stats, sums.T)
    return (attended, grad_tokens)


def solution(mesh):
    fine = Mesh(mesh.devices.reshape(2, 8, 2, 2, 8), ("xh", "y", "c", "xl", "z"))
    dp, mp = ("xh", "y", "c"), ("xl", "z")
    return jax.shard_map(
        per_device,
        mesh=fine,
        in_specs=(P(dp, mp), P(mp), P(None, dp, mp), P(), P(dp, mp)),
        out_specs=(P(dp, mp), P(dp, mp)),
        check_vma=False,
    )
```

```python
import jax
import jax.numpy as jnp
from jax import lax
from jax.experimental import pallas as pl
from jax.experimental.pallas import tpu as pltpu
from jax.sharding import Mesh, PartitionSpec as P

HEADSZ = 128
PATCH = 256
EPS = 1e-06
GAIN_ROWS = 16
F32 = jnp.float32
BF16 = jnp.bfloat16
VMEM = pl.BlockSpec(memory_space=pltpu.VMEM)
SMEM = pl.BlockSpec(memory_space=pltpu.SMEM)


def params(mib):
    return pltpu.CompilerParams(vmem_limit_bytes=mib * 1024 * 1024)


def dot(a, b, ca, cb):
    return lax.dot_general(a, b, (((ca,), (cb,)), ((), ())), preferred_element_type=F32)


def lane_fold(x):
    total = x[:, :128]
    for at in range(128, x.shape[1], 128):
        total = total + x[:, at : at + 128]
    return total


def normalise_kernel(feat_all, z_ref, *refs):
    pieces = refs[:-2]
    normed_ref, stat_ref = refs[-2:]
    z = z_ref[0]
    zs = 8
    blocks = []
    own = pieces[0]
    for xl in range(2):
        blocks.append((own, xl, xl * zs + z))
    for step in range(1, 4):
        for xl in range(2):
            blocks.append((pieces[2 * step - 1], xl, xl * zs + lax.rem(z + zs - step, zs)))
            blocks.append((pieces[2 * step], xl, xl * zs + lax.rem(z + step, zs)))
    far = lax.rem(z + 4, zs)
    blocks.append((pieces[7], 0, far))
    blocks.append((pieces[8], 0, zs + far))
    rows = PATCH
    total = jnp.zeros((rows, 128), F32)
    for ref, at, _ in blocks:
        total = total + lane_fold(ref[at, :rows, :].astype(F32))
    mean = jnp.sum(total, axis=1, keepdims=True) / feat_all
    total = jnp.zeros((rows, 128), F32)
    for ref, at, _ in blocks:
        centred = ref[at, :rows, :].astype(F32) - mean
        total = total + lane_fold(centred * centred)
    inv = lax.rsqrt(jnp.sum(total, axis=1, keepdims=True) / feat_all + EPS)
    for ref, at, place in blocks:
        x_hat = (ref[at, :rows, :].astype(F32) - mean) * inv
        gain = ref[at, rows : rows + 1, :].astype(F32)
        normed_ref[place, :rows, :] = (x_hat * gain).astype(BF16)
        normed_ref[place, rows:, :] = ref[at, rows:, :]
    stat_ref[0] = jnp.broadcast_to(mean, (rows, 128))
    stat_ref[1] = jnp.broadcast_to(inv, (rows, 128))


def norm128(x):
    mean = jnp.mean(x, axis=1, keepdims=True)
    centred = x - mean
    inv = lax.rsqrt(jnp.mean(centred * centred, axis=1, keepdims=True) + EPS)
    return centred * inv, inv


def norm128_back(grad_hat, x_hat, inv):
    first = jnp.mean(grad_hat, axis=1, keepdims=True)
    second = jnp.mean(grad_hat * x_hat, axis=1, keepdims=True)
    return inv * (grad_hat - first - x_hat * second)


def attention_kernel(normed_ref, w_ref, qk_ref, cot_ref, out_ref, grads_ref, sums_ref, acc):
    n_m = normed_ref.shape[0]
    third = w_ref.shape[2] // 3
    width = w_ref.shape[3]
    heads = width // HEADSZ
    acc[...] = jnp.zeros_like(acc)

    def step(m, carry):
        xh = m // 8
        y = lax.rem(m, 8)
        x = normed_ref[m]
        for i in range(3):
            w = jnp.concatenate(
                [w_ref[2 * y + c, xh, i * third : (i + 1) * third, :] for c in range(2)], axis=0
            )
            acc[:, i * width : (i + 1) * width] += dot(x, w, 1, 0)
        return carry

    lax.fori_loop(0, n_m, step, 0)
    rows = PATCH
    scale = HEADSZ ** (-0.5)
    gain_q = qk_ref[0:1, :]
    gain_k = qk_ref[1:2, :]
    first = jnp.zeros((rows, 128), F32)
    second = jnp.zeros((rows, 128), F32)
    for h in range(heads):
        cols = [slice(i * width + h * HEADSZ, i * width + (h + 1) * HEADSZ) for i in range(3)]
        own = slice(h * HEADSZ, (h + 1) * HEADSZ)
        proj = [acc[:rows, c] for c in cols]
        q_hat, q_inv = norm128(proj[0])
        k_hat, k_inv = norm128(proj[1])
        queries = (q_hat * gain_q).astype(BF16)
        keys = (k_hat * gain_k).astype(BF16)
        values = proj[2].astype(BF16)
        expo = jnp.exp(dot(queries, keys, 1, 1) * scale)
        probs = expo / jnp.sum(expo, axis=1, keepdims=True)
        weights_b = probs.astype(BF16)
        out_ref[:, own] = dot(weights_b, values, 1, 0).astype(BF16)
        upstream = cot_ref[:, own]
        d_probs = dot(upstream, values, 1, 1)
        d_values = dot(weights_b, upstream, 0, 0).astype(BF16)
        inner = jnp.sum(probs * d_probs, axis=1, keepdims=True)
        d_scores = (probs * (d_probs - inner) * scale).astype(BF16)
        d_queries = dot(d_scores, keys, 1, 0)
        d_keys = dot(d_scores, queries, 0, 0)
        grad_q = norm128_back(d_queries * gain_q, q_hat, q_inv).astype(BF16)
        grad_k = norm128_back(d_keys * gain_k, k_hat, k_inv).astype(BF16)
        for i, grad in enumerate((grad_q, grad_k, d_values)):
            grads_ref[i, :, own] = grad
            wide = grad.astype(F32)
            first = first + wide * acc[rows : rows + 1, cols[i]]
            second = second + wide * proj[i]
    sums_ref[...] = jnp.zeros_like(sums_ref)
    sums_ref[0:1, :rows] = jnp.sum(first, axis=1)[None, :]
    sums_ref[1:2, :rows] = jnp.sum(second, axis=1)[None, :]


def split_sums(sums):
    high = sums.astype(BF16).astype(F32)
    return jnp.concatenate([high, sums - high], axis=0).astype(BF16)


def join_sums(rows):
    wide = rows.astype(F32)
    return wide[:8] + wide[8:]


def backward_kernel(plan, z_ref, grads_ref, w_ref, sums_ref, *out_refs):
    third = w_ref.shape[2] // 3
    rows = PATCH
    tail = split_sums(sums_ref[...])
    for out_ref, places in zip(out_refs, plan):
        for at, (xl, offset) in enumerate(places):
            y = lax.rem(z_ref[0] + offset, 8)
            total = None
            for i in range(3):
                w = jnp.concatenate(
                    [w_ref[2 * y + c, xl, i * third : (i + 1) * third, :] for c in range(2)], axis=0
                )
                term = dot(grads_ref[i], w, 1, 1)
                total = term if total is None else total + term
            out_ref[at, :rows, :] = total.astype(BF16)
            out_ref[at, rows:, :] = tail


def add_kernel(first, got_ref, part_ref, out_ref):
    rows = PATCH
    for at in range(part_ref.shape[0]):
        if first <= at < first + got_ref.shape[0]:
            got = at - first
            out_ref[at, :rows, :] = (
                got_ref[got, :rows, :].astype(F32) + part_ref[at, :rows, :].astype(F32)
            ).astype(BF16)
            out_ref[at, rows:, :] = split_sums(
                join_sums(got_ref[got, rows:, :]) + join_sums(part_ref[at, rows:, :])
            )
        else:
            out_ref[at] = part_ref[at]


def join_kernel(xl_ref, ahead_ref, behind_ref, own_ref, mine_ref, other_ref):
    rows = PATCH
    for ref, at in ((mine_ref, xl_ref[0]), (other_ref, 1 - xl_ref[0])):
        refs = (ahead_ref, behind_ref, own_ref)
        total = sum(r[at, :rows, :].astype(F32) for r in refs)
        ref[:rows, :] = total.astype(BF16)
        ref[rows:, :] = split_sums(sum(join_sums(r[at, rows:, :]) for r in refs))


def final_kernel(feat_all, mine_ref, other_ref, tok_ref, gain_ref, stat_ref, out_ref):
    rows = PATCH
    b = mine_ref[:rows, :].astype(F32) + other_ref[:rows, :].astype(F32)
    b = b * gain_ref[0:1, :].astype(F32)
    sums = join_sums(mine_ref[rows:, :]) + join_sums(other_ref[rows:, :])
    diagonal = lax.broadcasted_iota(jnp.int32, (rows, rows), 0) == lax.broadcasted_iota(
        jnp.int32, (rows, rows), 1
    )
    first, second = (
        jnp.sum(jnp.where(diagonal, sums[i : i + 1, :rows], 0.0), axis=1, keepdims=True) / feat_all
        for i in range(2)
    )
    mean = stat_ref[0, :, 0:1]
    inv = stat_ref[1, :, 0:1]
    x_hat = (tok_ref[...].astype(F32) - mean) * inv
    out_ref[...] = (inv * (b - first - x_hat * second)).astype(BF16)


def ring(n, step):
    return [(i, (i + step) % n) for i in range(n)]


def per_device(tokens, ln_gain, qkv_weight, qk_gain, cotangent):
    rows, feat = tokens.shape
    width = qkv_weight.shape[2]
    feat_all = feat * 16
    z = lax.axis_index("z").astype(jnp.int32)

    weights = qkv_weight.reshape(-1, width)
    weights = lax.all_gather(weights, "xh", axis=0)
    weights = lax.all_gather(weights, ("y", "c"), axis=0)

    gain = jnp.broadcast_to(ln_gain[None, :], (GAIN_ROWS, feat))
    own = lax.all_gather(jnp.concatenate([tokens, gain], axis=0), "xl", axis=0)
    pieces = [own]
    ahead = behind = own
    for _ in range(3):
        ahead = lax.ppermute(ahead, "z", ring(8, 1))
        behind = lax.ppermute(behind, "z", ring(8, -1))
        pieces += [ahead, behind]
    pieces.append(lax.ppermute(ahead[:1], "z", ring(8, 1)))
    pieces.append(lax.ppermute(behind[1:], "z", ring(8, -1)))

    normed, stats = pl.pallas_call(
        lambda *refs: normalise_kernel(feat_all, *refs),
        out_shape=(
            jax.ShapeDtypeStruct((16, rows + GAIN_ROWS, feat), BF16),
            jax.ShapeDtypeStruct((2, rows, 128), F32),
        ),
        in_specs=[SMEM] + [VMEM] * len(pieces),
        out_specs=(VMEM, VMEM),
        compiler_params=params(32),
        name="normalise",
    )(z[None], *pieces)

    attended, grads, sums = pl.pallas_call(
        attention_kernel,
        out_shape=(
            jax.ShapeDtypeStruct((rows, width), BF16),
            jax.ShapeDtypeStruct((3, rows, width), BF16),
            jax.ShapeDtypeStruct((8, feat), F32),
        ),
        in_specs=[VMEM] * 4,
        out_specs=(VMEM,) * 3,
        scratch_shapes=[pltpu.VMEM((rows + GAIN_ROWS, 3 * width), F32)],
        compiler_params=params(40),
        name="attention",
    )(normed, weights, qk_gain, cotangent)

    block = (rows + GAIN_ROWS, feat)

    def backward(plan, name):
        flops = 2 * rows * feat * 3 * width * sum(len(places) for places in plan)
        return pl.pallas_call(
            lambda *refs: backward_kernel(plan, *refs),
            out_shape=tuple(jax.ShapeDtypeStruct((len(p),) + block, BF16) for p in plan),
            in_specs=[SMEM] + [VMEM] * 3,
            out_specs=(VMEM,) * len(plan),
            compiler_params=params(32),
            cost_estimate=pl.CostEstimate(flops=flops, bytes_accessed=2 * 2**20, transcendentals=0),
            name=name,
        )(z[None], grads, weights, sums)

    def add(got, part, first, name):
        return pl.pallas_call(
            lambda *refs: add_kernel(first, *refs),
            out_shape=jax.ShapeDtypeStruct(part.shape, BF16),
            in_specs=[VMEM] * 2,
            out_specs=VMEM,
            cost_estimate=pl.CostEstimate(flops=10**6, bytes_accessed=2**20, transcendentals=0),
            name=name,
        )(got, part)

    ahead, behind = backward((((0, 4),), ((1, 4),)), "backward_far")
    near = [((0, off), (1, off)) for off in (3, 5, 2, 6, 1, 7, 0)]
    parts = backward(tuple(near), "backward_near")
    for step in range(3):
        ahead = lax.ppermute(ahead, "z", ring(8, 1))
        behind = lax.ppermute(behind, "z", ring(8, -1))
        ahead = add(ahead, parts[2 * step], 0, "add_ahead")
        behind = add(behind, parts[2 * step + 1], 1 if step == 0 else 0, "add_behind")
    ahead = lax.ppermute(ahead, "z", ring(8, 1))
    behind = lax.ppermute(behind, "z", ring(8, -1))
    mine, other = pl.pallas_call(
        join_kernel,
        out_shape=(jax.ShapeDtypeStruct(block, BF16),) * 2,
        in_specs=[SMEM] + [VMEM] * 3,
        out_specs=(VMEM, VMEM),
        name="join",
    )(lax.axis_index("xl").astype(jnp.int32)[None], ahead, behind, parts[6])
    other = lax.ppermute(other, "xl", ring(2, 1))
    grad_tokens = pl.pallas_call(
        lambda *refs: final_kernel(feat_all, *refs),
        out_shape=jax.ShapeDtypeStruct((rows, feat), BF16),
        in_specs=[VMEM] * 5,
        out_specs=VMEM,
        name="final_norm",
    )(mine, other, tokens, gain, stats)
    return (attended, grad_tokens)


def solution(mesh):
    fine = Mesh(mesh.devices.reshape(2, 8, 2, 2, 8), ("xh", "y", "c", "xl", "z"))
    dp, mp = ("xh", "y", "c"), ("xl", "z")
    return jax.shard_map(
        per_device,
        mesh=fine,
        in_specs=(P(dp, mp), P(mp), P(None, dp, mp), P(), P(dp, mp)),
        out_specs=(P(dp, mp), P(dp, mp)),
        check_vma=False,
    )
```

```python
import jax
import jax.numpy as jnp
from jax import lax
from jax.experimental import pallas as pl
from jax.experimental.pallas import tpu as pltpu
from jax.sharding import Mesh, PartitionSpec as P

HEADSZ = 128
PATCH = 256
EPS = 1e-06
GAIN_ROWS = 16
F32 = jnp.float32
BF16 = jnp.bfloat16
VMEM = pl.BlockSpec(memory_space=pltpu.VMEM)
SMEM = pl.BlockSpec(memory_space=pltpu.SMEM)


def params(mib):
    return pltpu.CompilerParams(vmem_limit_bytes=mib * 1024 * 1024)


def dot(a, b, ca, cb):
    return lax.dot_general(a, b, (((ca,), (cb,)), ((), ())), preferred_element_type=F32)


def lane_fold(x):
    total = x[:, :128]
    for at in range(128, x.shape[1], 128):
        total = total + x[:, at : at + 128]
    return total


def normalise_kernel(feat_all, z_ref, *refs):
    pieces = refs[:-2]
    normed_ref, stat_ref = refs[-2:]
    z = z_ref[0]
    zs = 8
    blocks = []
    own = pieces[0]
    for xl in range(2):
        blocks.append((own, xl, xl * zs + z))
    for step in range(1, 4):
        for xl in range(2):
            blocks.append((pieces[2 * step - 1], xl, xl * zs + lax.rem(z + zs - step, zs)))
            blocks.append((pieces[2 * step], xl, xl * zs + lax.rem(z + step, zs)))
    far = lax.rem(z + 4, zs)
    blocks.append((pieces[7], 0, far))
    blocks.append((pieces[8], 0, zs + far))
    rows = PATCH
    total = jnp.zeros((rows, 128), F32)
    for ref, at, _ in blocks:
        total = total + lane_fold(ref[at, :rows, :].astype(F32))
    mean = jnp.sum(total, axis=1, keepdims=True) / feat_all
    total = jnp.zeros((rows, 128), F32)
    for ref, at, _ in blocks:
        centred = ref[at, :rows, :].astype(F32) - mean
        total = total + lane_fold(centred * centred)
    inv = lax.rsqrt(jnp.sum(total, axis=1, keepdims=True) / feat_all + EPS)
    for ref, at, place in blocks:
        x_hat = (ref[at, :rows, :].astype(F32) - mean) * inv
        gain = ref[at, rows : rows + 1, :].astype(F32)
        normed_ref[place, :rows, :] = (x_hat * gain).astype(BF16)
        normed_ref[place, rows:, :] = ref[at, rows:, :]
    stat_ref[0] = jnp.broadcast_to(mean, (rows, 128))
    stat_ref[1] = jnp.broadcast_to(inv, (rows, 128))


def norm128(x):
    mean = jnp.mean(x, axis=1, keepdims=True)
    centred = x - mean
    inv = lax.rsqrt(jnp.mean(centred * centred, axis=1, keepdims=True) + EPS)
    return centred * inv, inv


def norm128_back(grad_hat, x_hat, inv):
    first = jnp.mean(grad_hat, axis=1, keepdims=True)
    second = jnp.mean(grad_hat * x_hat, axis=1, keepdims=True)
    return inv * (grad_hat - first - x_hat * second)


def attention_kernel(normed_ref, w_ref, qk_ref, cot_ref, out_ref, grads_ref, sums_ref, acc):
    n_m = normed_ref.shape[0]
    third = w_ref.shape[2] // 3
    width = w_ref.shape[3]
    heads = width // HEADSZ
    acc[...] = jnp.zeros_like(acc)

    def step(m, carry):
        xh = m // 8
        y = lax.rem(m, 8)
        x = normed_ref[m]
        for i in range(3):
            w = jnp.concatenate(
                [w_ref[2 * y + c, xh, i * third : (i + 1) * third, :] for c in range(2)], axis=0
            )
            acc[:, i * width : (i + 1) * width] += dot(x, w, 1, 0)
        return carry

    lax.fori_loop(0, n_m, step, 0)
    rows = PATCH
    scale = HEADSZ ** (-0.5)
    gain_q = qk_ref[0:1, :]
    gain_k = qk_ref[1:2, :]
    first = jnp.zeros((rows, 128), F32)
    second = jnp.zeros((rows, 128), F32)
    for h in range(heads):
        cols = [slice(i * width + h * HEADSZ, i * width + (h + 1) * HEADSZ) for i in range(3)]
        own = slice(h * HEADSZ, (h + 1) * HEADSZ)
        proj = [acc[:rows, c] for c in cols]
        q_hat, q_inv = norm128(proj[0])
        k_hat, k_inv = norm128(proj[1])
        queries = (q_hat * gain_q).astype(BF16)
        keys = (k_hat * gain_k).astype(BF16)
        values = proj[2].astype(BF16)
        expo = jnp.exp(dot(queries, keys, 1, 1) * scale)
        probs = expo / jnp.sum(expo, axis=1, keepdims=True)
        weights_b = probs.astype(BF16)
        out_ref[:, own] = dot(weights_b, values, 1, 0).astype(BF16)
        upstream = cot_ref[:, own]
        d_probs = dot(upstream, values, 1, 1)
        d_values = dot(weights_b, upstream, 0, 0).astype(BF16)
        inner = jnp.sum(probs * d_probs, axis=1, keepdims=True)
        d_scores = (probs * (d_probs - inner) * scale).astype(BF16)
        d_queries = dot(d_scores, keys, 1, 0)
        d_keys = dot(d_scores, queries, 0, 0)
        grad_q = norm128_back(d_queries * gain_q, q_hat, q_inv).astype(BF16)
        grad_k = norm128_back(d_keys * gain_k, k_hat, k_inv).astype(BF16)
        for i, grad in enumerate((grad_q, grad_k, d_values)):
            grads_ref[i, :, own] = grad
            wide = grad.astype(F32)
            first = first + wide * acc[rows : rows + 1, cols[i]]
            second = second + wide * proj[i]
    sums_ref[...] = jnp.zeros_like(sums_ref)
    sums_ref[0:1, :rows] = jnp.sum(first, axis=1)[None, :]
    sums_ref[1:2, :rows] = jnp.sum(second, axis=1)[None, :]


def split_sums(sums):
    high = sums.astype(BF16).astype(F32)
    return jnp.concatenate([high, sums - high], axis=0).astype(BF16)


def join_sums(rows):
    wide = rows.astype(F32)
    return wide[:8] + wide[8:]


def backward_kernel(plan, z_ref, grads_ref, w_ref, sums_ref, *out_refs):
    third = w_ref.shape[2] // 3
    rows = PATCH
    tail = split_sums(sums_ref[...])
    for out_ref, places in zip(out_refs, plan):
        for at, (xl, offset) in enumerate(places):
            y = lax.rem(z_ref[0] + offset, 8)
            total = None
            for i in range(3):
                w = jnp.concatenate(
                    [w_ref[2 * y + c, xl, i * third : (i + 1) * third, :] for c in range(2)], axis=0
                )
                term = dot(grads_ref[i], w, 1, 1)
                total = term if total is None else total + term
            out_ref[at, :rows, :] = total.astype(BF16)
            out_ref[at, rows:, :] = tail


def add_kernel(first, got_ref, part_ref, out_ref):
    rows = PATCH
    for at in range(part_ref.shape[0]):
        if first <= at < first + got_ref.shape[0]:
            got = at - first
            out_ref[at, :rows, :] = (
                got_ref[got, :rows, :].astype(F32) + part_ref[at, :rows, :].astype(F32)
            ).astype(BF16)
            out_ref[at, rows:, :] = split_sums(
                join_sums(got_ref[got, rows:, :]) + join_sums(part_ref[at, rows:, :])
            )
        else:
            out_ref[at] = part_ref[at]


def join_kernel(xl_ref, ahead_ref, behind_ref, own_ref, mine_ref, other_ref):
    rows = PATCH
    for ref, at in ((mine_ref, xl_ref[0]), (other_ref, 1 - xl_ref[0])):
        refs = (ahead_ref, behind_ref, own_ref)
        total = sum(r[at, :rows, :].astype(F32) for r in refs)
        ref[:rows, :] = total.astype(BF16)
        ref[rows:, :] = split_sums(sum(join_sums(r[at, rows:, :]) for r in refs))


def final_kernel(feat_all, mine_ref, other_ref, tok_ref, gain_ref, stat_ref, out_ref):
    rows = PATCH
    b = mine_ref[:rows, :].astype(F32) + other_ref[:rows, :].astype(F32)
    b = b * gain_ref[0:1, :].astype(F32)
    sums = join_sums(mine_ref[rows:, :]) + join_sums(other_ref[rows:, :])
    diagonal = lax.broadcasted_iota(jnp.int32, (rows, rows), 0) == lax.broadcasted_iota(
        jnp.int32, (rows, rows), 1
    )
    first, second = (
        jnp.sum(jnp.where(diagonal, sums[i : i + 1, :rows], 0.0), axis=1, keepdims=True) / feat_all
        for i in range(2)
    )
    mean = stat_ref[0, :, 0:1]
    inv = stat_ref[1, :, 0:1]
    x_hat = (tok_ref[...].astype(F32) - mean) * inv
    out_ref[...] = (inv * (b - first - x_hat * second)).astype(BF16)


def ring(n, step):
    return [(i, (i + step) % n) for i in range(n)]


def per_device(tokens, ln_gain, qkv_weight, qk_gain, cotangent):
    rows, feat = tokens.shape
    width = qkv_weight.shape[2]
    feat_all = feat * 16
    z = lax.axis_index("z").astype(jnp.int32)

    weights = qkv_weight.reshape(-1, width)
    weights = lax.all_gather(weights, "xh", axis=0)
    weights = lax.all_gather(weights, ("y", "c"), axis=0)

    gain = jnp.broadcast_to(ln_gain[None, :], (GAIN_ROWS, feat))
    own = lax.all_gather(jnp.concatenate([tokens, gain], axis=0), "xl", axis=0)
    pieces = [own]
    ahead = behind = own
    for _ in range(3):
        ahead = lax.ppermute(ahead, "z", ring(8, 1))
        behind = lax.ppermute(behind, "z", ring(8, -1))
        pieces += [ahead, behind]
    pieces.append(lax.ppermute(ahead[:1], "z", ring(8, 1)))
    pieces.append(lax.ppermute(behind[1:], "z", ring(8, -1)))

    normed, stats = pl.pallas_call(
        lambda *refs: normalise_kernel(feat_all, *refs),
        out_shape=(
            jax.ShapeDtypeStruct((16, rows + GAIN_ROWS, feat), BF16),
            jax.ShapeDtypeStruct((2, rows, 128), F32),
        ),
        in_specs=[SMEM] + [VMEM] * len(pieces),
        out_specs=(VMEM, VMEM),
        compiler_params=params(16),
        name="normalise",
    )(z[None], *pieces)

    attended, grads, sums = pl.pallas_call(
        attention_kernel,
        out_shape=(
            jax.ShapeDtypeStruct((rows, width), BF16),
            jax.ShapeDtypeStruct((3, rows, width), BF16),
            jax.ShapeDtypeStruct((8, feat), F32),
        ),
        in_specs=[VMEM] * 4,
        out_specs=(VMEM,) * 3,
        scratch_shapes=[pltpu.VMEM((rows + GAIN_ROWS, 3 * width), F32)],
        compiler_params=params(16),
        name="attention",
    )(normed, weights, qk_gain, cotangent)

    block = (rows + GAIN_ROWS, feat)

    def backward(plan, name):
        flops = 2 * rows * feat * 3 * width * sum(len(places) for places in plan)
        return pl.pallas_call(
            lambda *refs: backward_kernel(plan, *refs),
            out_shape=tuple(jax.ShapeDtypeStruct((len(p),) + block, BF16) for p in plan),
            in_specs=[SMEM] + [VMEM] * 3,
            out_specs=(VMEM,) * len(plan),
            compiler_params=params(16),
            cost_estimate=pl.CostEstimate(flops=flops, bytes_accessed=2 * 2**20, transcendentals=0),
            name=name,
        )(z[None], grads, weights, sums)

    def add(got, part, first, name):
        return pl.pallas_call(
            lambda *refs: add_kernel(first, *refs),
            out_shape=jax.ShapeDtypeStruct(part.shape, BF16),
            in_specs=[VMEM] * 2,
            out_specs=VMEM,
            compiler_params=params(16),
            cost_estimate=pl.CostEstimate(flops=10**6, bytes_accessed=2**20, transcendentals=0),
            name=name,
        )(got, part)

    ahead, behind = backward((((0, 4),), ((1, 4),)), "backward_far")
    near = [((0, off), (1, off)) for off in (3, 5, 2, 6, 1, 7, 0)]
    parts = backward(tuple(near), "backward_near")
    for step in range(3):
        ahead = lax.ppermute(ahead, "z", ring(8, 1))
        behind = lax.ppermute(behind, "z", ring(8, -1))
        ahead = add(ahead, parts[2 * step], 0, "add_ahead")
        behind = add(behind, parts[2 * step + 1], 1 if step == 0 else 0, "add_behind")
    ahead = lax.ppermute(ahead, "z", ring(8, 1))
    behind = lax.ppermute(behind, "z", ring(8, -1))
    mine, other = pl.pallas_call(
        join_kernel,
        out_shape=(jax.ShapeDtypeStruct(block, BF16),) * 2,
        in_specs=[SMEM] + [VMEM] * 3,
        out_specs=(VMEM, VMEM),
        compiler_params=params(16),
        name="join",
    )(lax.axis_index("xl").astype(jnp.int32)[None], ahead, behind, parts[6])
    other = lax.ppermute(other, "xl", ring(2, 1))
    grad_tokens = pl.pallas_call(
        lambda *refs: final_kernel(feat_all, *refs),
        out_shape=jax.ShapeDtypeStruct((rows, feat), BF16),
        in_specs=[VMEM] * 5,
        out_specs=VMEM,
        compiler_params=params(16),
        name="final_norm",
    )(mine, other, tokens, gain, stats)
    return (attended, grad_tokens)


def solution(mesh):
    fine = Mesh(mesh.devices.reshape(2, 8, 2, 2, 8), ("xh", "y", "c", "xl", "z"))
    dp, mp = ("xh", "y", "c"), ("xl", "z")
    return jax.shard_map(
        per_device,
        mesh=fine,
        in_specs=(P(dp, mp), P(mp), P(None, dp, mp), P(), P(dp, mp)),
        out_specs=(P(dp, mp), P(dp, mp)),
        check_vma=False,
    )
```

```python
import jax
import jax.numpy as jnp
from jax import lax
from jax.experimental import pallas as pl
from jax.experimental.pallas import tpu as pltpu
from jax.sharding import Mesh, PartitionSpec as P

HEADSZ = 128
PATCH = 256
EPS = 1e-06
GAIN_ROWS = 16
F32 = jnp.float32
BF16 = jnp.bfloat16
VMEM = pl.BlockSpec(memory_space=pltpu.VMEM)
HBM = pl.BlockSpec(memory_space=pltpu.HBM)


def params(mib):
    return pltpu.CompilerParams(vmem_limit_bytes=mib * 1024 * 1024)


def dot(a, b, ca, cb):
    return lax.dot_general(a, b, (((ca,), (cb,)), ((), ())), preferred_element_type=F32)


def lane_fold(x):
    total = x[:, :128]
    for at in range(128, x.shape[1], 128):
        total = total + x[:, at : at + 128]
    return total


def normalise_kernel(feat_all, offsets, which, *refs):
    pieces = refs[:-2]
    normed_ref, stat_ref = refs[-2:]
    rows = PATCH
    blocks = []
    for ref, offset, kinds in zip(pieces, offsets, which):
        for at, xl in enumerate(kinds):
            blocks.append((ref, at, xl * 8 + lax.rem(lax.axis_index("z") + offset, 8)))
    total = jnp.zeros((rows, 128), F32)
    for ref, at, _ in blocks:
        total = total + lane_fold(ref[at, :rows, :].astype(F32))
    mean = jnp.sum(total, axis=1, keepdims=True) / feat_all
    total = jnp.zeros((rows, 128), F32)
    for ref, at, _ in blocks:
        centred = ref[at, :rows, :].astype(F32) - mean
        total = total + lane_fold(centred * centred)
    inv = lax.rsqrt(jnp.sum(total, axis=1, keepdims=True) / feat_all + EPS)
    for ref, at, place in blocks:
        x_hat = (ref[at, :rows, :].astype(F32) - mean) * inv
        gain = ref[at, rows : rows + 1, :].astype(F32)
        normed_ref[place, :rows, :] = (x_hat * gain).astype(BF16)
        normed_ref[place, rows:, :] = ref[at, rows:, :]
    stat_ref[0] = jnp.broadcast_to(mean, (rows, 128))
    stat_ref[1] = jnp.broadcast_to(inv, (rows, 128))


def weight_block(w_ref, m, i):
    third = w_ref.shape[2] // 3
    return jnp.concatenate([w_ref[c, m, i * third : (i + 1) * third, :] for c in range(2)], axis=0)


def norm128(x):
    mean = jnp.mean(x, axis=1, keepdims=True)
    centred = x - mean
    inv = lax.rsqrt(jnp.mean(centred * centred, axis=1, keepdims=True) + EPS)
    return centred * inv, inv


def norm128_back(grad_hat, x_hat, inv):
    first = jnp.mean(grad_hat, axis=1, keepdims=True)
    second = jnp.mean(grad_hat * x_hat, axis=1, keepdims=True)
    return inv * (grad_hat - first - x_hat * second)


def split_sums(sums):
    high = sums.astype(BF16).astype(F32)
    return jnp.concatenate([high, sums - high], axis=0).astype(BF16)


def join_sums(rows):
    wide = rows.astype(F32)
    return wide[:8] + wide[8:]


def core_kernel(plan, normed_hbm, w_hbm, qk_hbm, cot_hbm, *refs):
    out_ref = refs[0]
    part_refs = refs[1 : 1 + len(plan)]
    w_ref, normed_ref, qk_ref, cot_ref, acc, grads_ref, sems, small_sems = refs[1 + len(plan) :]
    width = w_ref.shape[3]
    heads = width // HEADSZ
    n_m = normed_ref.shape[0]

    def copies(m):
        x_hi, y = divmod(m, 8)
        found = [pltpu.make_async_copy(normed_hbm.at[m], normed_ref.at[m], sems.at[m, 2])]
        for c in range(2):
            found.append(
                pltpu.make_async_copy(w_hbm.at[2 * y + c, x_hi], w_ref.at[c, m], sems.at[m, c])
            )
        return found

    small = [
        pltpu.make_async_copy(qk_hbm, qk_ref, small_sems.at[0]),
        pltpu.make_async_copy(cot_hbm, cot_ref, small_sems.at[1]),
    ]
    for m in range(n_m):
        for copy in copies(m):
            copy.start()
    for copy in small:
        copy.start()
    for m in range(n_m):
        for copy in copies(m):
            copy.wait()
        x = normed_ref[m]
        for i in range(3):
            term = dot(x, weight_block(w_ref, m, i), 1, 0)
            at = slice(i * width, (i + 1) * width)
            acc[:, at] = term if m == 0 else acc[:, at] + term
    for copy in small:
        copy.wait()
    rows = PATCH
    scale = HEADSZ ** (-0.5)
    gain_q = qk_ref[0:1, :]
    gain_k = qk_ref[1:2, :]
    first = jnp.zeros((rows, 128), F32)
    second = jnp.zeros((rows, 128), F32)
    for h in range(heads):
        cols = [slice(i * width + h * HEADSZ, i * width + (h + 1) * HEADSZ) for i in range(3)]
        own = slice(h * HEADSZ, (h + 1) * HEADSZ)
        proj = [acc[:rows, c] for c in cols]
        q_hat, q_inv = norm128(proj[0])
        k_hat, k_inv = norm128(proj[1])
        queries = (q_hat * gain_q).astype(BF16)
        keys = (k_hat * gain_k).astype(BF16)
        values = proj[2].astype(BF16)
        expo = jnp.exp(dot(queries, keys, 1, 1) * scale)
        probs = expo / jnp.sum(expo, axis=1, keepdims=True)
        weights_b = probs.astype(BF16)
        out_ref[:, own] = dot(weights_b, values, 1, 0).astype(BF16)
        upstream = cot_ref[:, own]
        d_probs = dot(upstream, values, 1, 1)
        d_values = dot(weights_b, upstream, 0, 0).astype(BF16)
        inner = jnp.sum(probs * d_probs, axis=1, keepdims=True)
        d_scores = (probs * (d_probs - inner) * scale).astype(BF16)
        d_queries = dot(d_scores, keys, 1, 0)
        d_keys = dot(d_scores, queries, 0, 0)
        grad_q = norm128_back(d_queries * gain_q, q_hat, q_inv).astype(BF16)
        grad_k = norm128_back(d_keys * gain_k, k_hat, k_inv).astype(BF16)
        for i, grad in enumerate((grad_q, grad_k, d_values)):
            grads_ref[i, :, own] = grad
            wide = grad.astype(F32)
            first = first + wide * acc[rows : rows + 1, cols[i]]
            second = second + wide * proj[i]
    sums = jnp.concatenate(
        [
            jnp.sum(first, axis=1)[None, :],
            jnp.sum(second, axis=1)[None, :],
            jnp.zeros((6, rows), F32),
        ],
        axis=0,
    )
    tail = split_sums(sums)
    for part_ref, places in zip(part_refs, plan):
        for at, (xl, offset) in enumerate(places):
            m = xl * 8 + lax.rem(lax.axis_index("z") + offset, 8)
            total = None
            for i in range(3):
                term = dot(grads_ref[i], weight_block(w_ref, m, i), 1, 1)
                total = term if total is None else total + term
            part_ref[at, :rows, :] = total.astype(BF16)
            part_ref[at, rows:, :rows] = tail
            part_ref[at, rows:, rows:] = jnp.zeros((GAIN_ROWS, total.shape[1] - rows), BF16)


def add_kernel(first, got_ref, part_ref, out_ref):
    rows = PATCH
    for at in range(part_ref.shape[0]):
        if first <= at < first + got_ref.shape[0]:
            got = at - first
            out_ref[at, :rows, :] = (
                got_ref[got, :rows, :].astype(F32) + part_ref[at, :rows, :].astype(F32)
            ).astype(BF16)
            out_ref[at, rows:, :] = split_sums(
                join_sums(got_ref[got, rows:, :]) + join_sums(part_ref[at, rows:, :])
            )
        else:
            out_ref[at] = part_ref[at]


def join_kernel(ahead_ref, behind_ref, own_ref, mine_ref, other_ref):
    rows = PATCH
    xl = lax.axis_index("xl")
    for ref, at in ((mine_ref, xl), (other_ref, 1 - xl)):
        refs = (ahead_ref, behind_ref, own_ref)
        total = sum(r[at, :rows, :].astype(F32) for r in refs)
        ref[:rows, :] = total.astype(BF16)
        ref[rows:, :] = split_sums(sum(join_sums(r[at, rows:, :]) for r in refs))


def final_kernel(feat_all, mine_ref, other_ref, tok_ref, gain_ref, stat_ref, out_ref):
    rows = PATCH
    b = mine_ref[:rows, :].astype(F32) + other_ref[:rows, :].astype(F32)
    b = b * gain_ref[0:1, :].astype(F32)
    sums = join_sums(mine_ref[rows:, :]) + join_sums(other_ref[rows:, :])
    diagonal = lax.broadcasted_iota(jnp.int32, (rows, rows), 0) == lax.broadcasted_iota(
        jnp.int32, (rows, rows), 1
    )
    first, second = (
        jnp.sum(jnp.where(diagonal, sums[i : i + 1, :rows], 0.0), axis=1, keepdims=True) / feat_all
        for i in range(2)
    )
    mean = stat_ref[0, :, 0:1]
    inv = stat_ref[1, :, 0:1]
    x_hat = (tok_ref[...].astype(F32) - mean) * inv
    out_ref[...] = (inv * (b - first - x_hat * second)).astype(BF16)


def ring(n, step):
    return [(i, (i + step) % n) for i in range(n)]


def per_device(tokens, ln_gain, qkv_weight, qk_gain, cotangent):
    rows, feat = tokens.shape
    width = qkv_weight.shape[2]
    feat_all = feat * 16

    weights = lax.all_gather(qkv_weight.reshape(-1, width), "xh", axis=0)
    weights = lax.all_gather(weights, ("y", "c"), axis=0)

    gain = jnp.broadcast_to(ln_gain[None, :], (GAIN_ROWS, feat))
    toks = lax.all_gather(jnp.concatenate([tokens, gain], axis=0), "xl", axis=0)
    pieces = [toks]
    ahead = behind = toks
    for _ in range(3):
        ahead = lax.ppermute(ahead, "z", ring(8, 1))
        behind = lax.ppermute(behind, "z", ring(8, -1))
        pieces += [ahead, behind]
    pieces.append(lax.ppermute(ahead[:1], "z", ring(8, 1)))
    pieces.append(lax.ppermute(behind[1:], "z", ring(8, -1)))
    places = (0, 7, 1, 6, 2, 5, 3, 4, 4)
    which = ((0, 1),) * 7 + ((0,), (1,))

    normed, stats = pl.pallas_call(
        lambda *refs: normalise_kernel(feat_all, places, which, *refs),
        out_shape=(
            jax.ShapeDtypeStruct((16, rows + GAIN_ROWS, feat), BF16),
            jax.ShapeDtypeStruct((2, rows, 128), F32),
        ),
        in_specs=[VMEM] * len(pieces),
        out_specs=(VMEM, VMEM),
        compiler_params=params(16),
        name="normalise",
    )(*pieces)

    block = (rows + GAIN_ROWS, feat)
    near = [((0, off), (1, off)) for off in (3, 5, 2, 6, 1, 7, 0)]
    plan = [((0, 4),), ((1, 4),)] + near
    attended, ahead, behind, *parts = pl.pallas_call(
        lambda *refs: core_kernel(plan, *refs),
        out_shape=(
            jax.ShapeDtypeStruct((rows, width), BF16),
            *(jax.ShapeDtypeStruct((len(p),) + block, BF16) for p in plan),
        ),
        in_specs=[HBM] * 4,
        out_specs=(VMEM,) * (1 + len(plan)),
        scratch_shapes=[
            pltpu.VMEM((2, 16) + weights.shape[2:], BF16),
            pltpu.VMEM(normed.shape, BF16),
            pltpu.VMEM(qk_gain.shape, F32),
            pltpu.VMEM(cotangent.shape, BF16),
            pltpu.VMEM((rows + GAIN_ROWS, 3 * width), F32),
            pltpu.VMEM((3, rows, width), BF16),
            pltpu.SemaphoreType.DMA((16, 3)),
            pltpu.SemaphoreType.DMA((2,)),
        ],
        compiler_params=params(50),
        name="core",
    )(normed, weights, qk_gain, cotangent)

    def add(got, part, first, name):
        return pl.pallas_call(
            lambda *refs: add_kernel(first, *refs),
            out_shape=jax.ShapeDtypeStruct(part.shape, BF16),
            in_specs=[VMEM] * 2,
            out_specs=VMEM,
            compiler_params=params(16),
            cost_estimate=pl.CostEstimate(flops=10**6, bytes_accessed=2**20, transcendentals=0),
            name=name,
        )(got, part)

    for step in range(3):
        ahead = lax.ppermute(ahead, "z", ring(8, 1))
        behind = lax.ppermute(behind, "z", ring(8, -1))
        ahead = add(ahead, parts[2 * step], 0, "add_ahead")
        behind = add(behind, parts[2 * step + 1], 1 if step == 0 else 0, "add_behind")
    ahead = lax.ppermute(ahead, "z", ring(8, 1))
    behind = lax.ppermute(behind, "z", ring(8, -1))
    mine, other = pl.pallas_call(
        join_kernel,
        out_shape=(jax.ShapeDtypeStruct(block, BF16),) * 2,
        in_specs=[VMEM] * 3,
        out_specs=(VMEM, VMEM),
        compiler_params=params(16),
        name="join",
    )(ahead, behind, parts[6])
    other = lax.ppermute(other, "xl", ring(2, 1))
    grad_tokens = pl.pallas_call(
        lambda *refs: final_kernel(feat_all, *refs),
        out_shape=jax.ShapeDtypeStruct((rows, feat), BF16),
        in_specs=[VMEM] * 5,
        out_specs=VMEM,
        compiler_params=params(16),
        name="final_norm",
    )(mine, other, tokens, gain, stats)
    return (attended, grad_tokens)


def solution(mesh):
    fine = Mesh(mesh.devices.reshape(2, 8, 2, 2, 8), ("xh", "y", "c", "xl", "z"))
    dp, mp = ("xh", "y", "c"), ("xl", "z")
    return jax.shard_map(
        per_device,
        mesh=fine,
        in_specs=(P(dp, mp), P(mp), P(None, dp, mp), P(), P(dp, mp)),
        out_specs=(P(dp, mp), P(dp, mp)),
        check_vma=False,
    )
```

```python
import jax
import jax.numpy as jnp
from jax import lax
from jax.experimental import pallas as pl
from jax.experimental.pallas import tpu as pltpu
from jax.sharding import Mesh, PartitionSpec as P

HEADSZ = 128
PATCH = 256
EPS = 1e-06
GAIN_ROWS = 16
F32 = jnp.float32
BF16 = jnp.bfloat16
VMEM = pl.BlockSpec(memory_space=pltpu.VMEM)
HBM = pl.BlockSpec(memory_space=pltpu.HBM)


def params(mib):
    return pltpu.CompilerParams(vmem_limit_bytes=mib * 1024 * 1024)


def dot(a, b, ca, cb):
    return lax.dot_general(a, b, (((ca,), (cb,)), ((), ())), preferred_element_type=F32)


def lane_fold(x):
    total = x[:, :128]
    for at in range(128, x.shape[1], 128):
        total = total + x[:, at : at + 128]
    return total


def normalise_kernel(feat_all, offsets, which, qk_ref, cot_ref, *refs):
    pieces = refs[:-2]
    normed_ref, stat_ref = refs[-2:]
    rows = PATCH
    blocks = []
    for ref, offset, kinds in zip(pieces, offsets, which):
        for at, xl in enumerate(kinds):
            blocks.append((ref, at, xl * 8 + lax.rem(lax.axis_index("z") + offset, 8)))
    total = jnp.zeros((rows, 128), F32)
    for ref, at, _ in blocks:
        total = total + lane_fold(ref[at, :rows, :].astype(F32))
    mean = jnp.sum(total, axis=1, keepdims=True) / feat_all
    total = jnp.zeros((rows, 128), F32)
    for ref, at, _ in blocks:
        centred = ref[at, :rows, :].astype(F32) - mean
        total = total + lane_fold(centred * centred)
    inv = lax.rsqrt(jnp.sum(total, axis=1, keepdims=True) / feat_all + EPS)
    for ref, at, place in blocks:
        x_hat = (ref[at, :rows, :].astype(F32) - mean) * inv
        gain = ref[at, rows : rows + 1, :].astype(F32)
        normed_ref[place, :rows, :] = (x_hat * gain).astype(BF16)
        normed_ref[place, rows:, :] = ref[at, rows:, :]
    normed_ref[16, :rows, :rows] = cot_ref[...]
    high = qk_ref[...].astype(BF16).astype(F32)
    middle = (qk_ref[...] - high).astype(BF16).astype(F32)
    low = qk_ref[...] - high - middle
    rest = jnp.zeros((GAIN_ROWS - 6, 128), F32)
    normed_ref[16, rows:, :128] = jnp.concatenate([high, middle, low, rest], axis=0).astype(BF16)
    stat_ref[0] = jnp.broadcast_to(mean, (rows, 128))
    stat_ref[1] = jnp.broadcast_to(inv, (rows, 128))


def weight_rows(blocks):
    third = blocks[0].shape[0] // 3
    return jnp.concatenate(
        [
            jnp.concatenate([w[i * third : (i + 1) * third, :] for w in blocks], axis=0)
            for i in range(3)
        ],
        axis=1,
    )


def norm128(x):
    mean = jnp.mean(x, axis=1, keepdims=True)
    centred = x - mean
    inv = lax.rsqrt(jnp.mean(centred * centred, axis=1, keepdims=True) + EPS)
    return centred * inv, inv


def norm128_back(grad_hat, x_hat, inv):
    first = jnp.mean(grad_hat, axis=1, keepdims=True)
    second = jnp.mean(grad_hat * x_hat, axis=1, keepdims=True)
    return inv * (grad_hat - first - x_hat * second)


def split_sums(sums):
    high = sums.astype(BF16).astype(F32)
    return jnp.concatenate([high, sums - high], axis=0).astype(BF16)


def join_sums(rows):
    wide = rows.astype(F32)
    return wide[:8] + wide[8:]


def backward(offsets, grads, tail, fetch, part_refs):
    rows = PATCH
    for offset, refs in zip(offsets, part_refs):
        total = dot(grads, weight_rows(fetch(offset)), 1, 1)
        feat = total.shape[1] // 2
        for xl, (ref, at) in enumerate(refs):
            ref[at, :rows, :] = total[:, xl * feat : (xl + 1) * feat].astype(BF16)
            ref[at, rows:, :rows] = tail
            ref[at, rows:, rows:] = jnp.zeros((GAIN_ROWS, feat - rows), BF16)


def core_kernel(
    normed_hbm,
    w_hbm,
    out_ref,
    far_ahead_ref,
    far_behind_ref,
    ahead_ref,
    behind_ref,
    grads_ref,
    tail_ref,
    w_ref,
    normed_ref,
    acc,
    sems,
):
    width = w_ref.shape[3]
    heads = width // HEADSZ
    n_m = w_ref.shape[1]

    def copies(m):
        x_hi, y = divmod(m, 8)
        found = [pltpu.make_async_copy(normed_hbm.at[m], normed_ref.at[m], sems.at[m, 2])]
        if m == n_m:
            return found
        for c in range(2):
            found.append(
                pltpu.make_async_copy(w_hbm.at[2 * y + c, x_hi], w_ref.at[c, m], sems.at[m, c])
            )
        return found

    for m in range(n_m + 1):
        for copy in copies(m):
            copy.start()
    for m in range(0, n_m, 2):
        for k in range(2):
            for copy in copies(m + k):
                copy.wait()
        x = jnp.concatenate([normed_ref[m], normed_ref[m + 1]], axis=1)
        term = dot(x, weight_rows([w_ref[c, m + k] for k in range(2) for c in range(2)]), 1, 0)
        acc[...] = term if m == 0 else acc[...] + term
    for copy in copies(n_m):
        copy.wait()
    gains = normed_ref[n_m, PATCH:, :HEADSZ].astype(F32)
    rows = PATCH
    scale = HEADSZ ** (-0.5)
    gain_q, gain_k = (gains[i : i + 1] + gains[i + 2 : i + 3] + gains[i + 4 : i + 5] for i in range(2))
    first = jnp.zeros((rows, 128), F32)
    second = jnp.zeros((rows, 128), F32)
    for h in range(heads):
        cols = [slice(i * width + h * HEADSZ, i * width + (h + 1) * HEADSZ) for i in range(3)]
        own = slice(h * HEADSZ, (h + 1) * HEADSZ)
        proj = [acc[:rows, c] for c in cols]
        q_hat, q_inv = norm128(proj[0])
        k_hat, k_inv = norm128(proj[1])
        queries = (q_hat * gain_q).astype(BF16)
        keys = (k_hat * gain_k).astype(BF16)
        values = proj[2].astype(BF16)
        expo = jnp.exp(dot(queries, keys, 1, 1) * scale)
        probs = expo / jnp.sum(expo, axis=1, keepdims=True)
        weights_b = probs.astype(BF16)
        out_ref[:, own] = dot(weights_b, values, 1, 0).astype(BF16)
        upstream = normed_ref[n_m, :rows, own]
        d_probs = dot(upstream, values, 1, 1)
        d_values = dot(weights_b, upstream, 0, 0).astype(BF16)
        inner = jnp.sum(probs * d_probs, axis=1, keepdims=True)
        d_scores = (probs * (d_probs - inner) * scale).astype(BF16)
        d_queries = dot(d_scores, keys, 1, 0)
        d_keys = dot(d_scores, queries, 0, 0)
        grad_q = norm128_back(d_queries * gain_q, q_hat, q_inv).astype(BF16)
        grad_k = norm128_back(d_keys * gain_k, k_hat, k_inv).astype(BF16)
        for i, grad in enumerate((grad_q, grad_k, d_values)):
            grads_ref[:, cols[i]] = grad
            wide = grad.astype(F32)
            first = first + wide * acc[rows : rows + 1, cols[i]]
            second = second + wide * proj[i]
    sums = jnp.concatenate(
        [
            jnp.sum(first, axis=1)[None, :],
            jnp.sum(second, axis=1)[None, :],
            jnp.zeros((6, rows), F32),
        ],
        axis=0,
    )
    tail = split_sums(sums)
    tail_ref[...] = tail

    def fetch(offset):
        y = lax.rem(lax.axis_index("z") + offset, 8)
        return [w_ref[c, xl * 8 + y] for xl in range(2) for c in range(2)]

    part_refs = [((far_ahead_ref, 0), (far_behind_ref, 0))]
    part_refs += [((ref, 0), (ref, 1)) for ref in (ahead_ref, behind_ref)]
    backward((4, 3, 5), grads_ref[...], tail, fetch, part_refs)


def rest_kernel(grads_ref, tail_ref, w_hbm, *refs):
    part_refs = refs[:4]
    mine_ref, other_ref, w_ref, own_ref, sems = refs[4:]
    offsets = (2, 6, 1, 7, 0)

    def copies(at):
        y = lax.rem(lax.axis_index("z") + offsets[at], 8)
        return [
            pltpu.make_async_copy(w_hbm.at[2 * y + c, xl], w_ref.at[at, c, xl], sems.at[at, c, xl])
            for xl in range(2)
            for c in range(2)
        ]

    def fetch(offset):
        at = offsets.index(offset)
        for copy in copies(at):
            copy.wait()
        return [w_ref[at, c, xl] for xl in range(2) for c in range(2)]

    for at in range(len(offsets)):
        for copy in copies(at):
            copy.start()
    places = [((ref, 0), (ref, 1)) for ref in (*part_refs, own_ref)]
    backward(offsets, grads_ref[...], tail_ref[...], fetch, places)
    xl = lax.axis_index("xl")
    mine_ref[...] = own_ref[xl]
    other_ref[...] = own_ref[1 - xl]


def add_kernel(first, got_ref, part_ref, *out_refs):
    rows = PATCH
    n = part_ref.shape[0]
    for k in range(n):
        if len(out_refs) == 1:
            at, store = k, out_refs[0].at[k]
        else:
            at, store = (lax.axis_index("xl") + k) % n, out_refs[k]
        if len(out_refs) > 1 or first <= at < first + got_ref.shape[0]:
            got = at - first
            store[:rows, :] = (
                got_ref[got, :rows, :].astype(F32) + part_ref[at, :rows, :].astype(F32)
            ).astype(BF16)
            store[rows:, :] = split_sums(
                join_sums(got_ref[got, rows:, :]) + join_sums(part_ref[at, rows:, :])
            )
        else:
            store[...] = part_ref[at]


def final_kernel(feat_all, tok_ref, gain_ref, stat_ref, *refs):
    rows = PATCH
    out_ref = refs[-1]
    b = sum(ref[:rows, :].astype(F32) for ref in refs[:-1])
    b = b * gain_ref[0:1, :].astype(F32)
    sums = sum(join_sums(ref[rows:, :]) for ref in refs[:-1])
    diagonal = lax.broadcasted_iota(jnp.int32, (rows, rows), 0) == lax.broadcasted_iota(
        jnp.int32, (rows, rows), 1
    )
    first, second = (
        jnp.sum(jnp.where(diagonal, sums[i : i + 1, :rows], 0.0), axis=1, keepdims=True) / feat_all
        for i in range(2)
    )
    mean = stat_ref[0, :, 0:1]
    inv = stat_ref[1, :, 0:1]
    x_hat = (tok_ref[...].astype(F32) - mean) * inv
    out_ref[...] = (inv * (b - first - x_hat * second)).astype(BF16)


def ring(n, step):
    return [(i, (i + step) % n) for i in range(n)]


def per_device(tokens, ln_gain, qkv_weight, qk_gain, cotangent):
    rows, feat = tokens.shape
    width = qkv_weight.shape[2]
    feat_all = feat * 16

    weights = lax.all_gather(qkv_weight.reshape(-1, width), "xh", axis=0)
    weights = lax.all_gather(weights, ("y", "c"), axis=0)

    gain = jnp.broadcast_to(ln_gain[None, :], (GAIN_ROWS, feat))
    toks = lax.all_gather(jnp.concatenate([tokens, gain], axis=0), "xl", axis=0)
    pieces = [toks]
    ahead = behind = toks
    for _ in range(3):
        ahead = lax.ppermute(ahead, "z", ring(8, 1))
        behind = lax.ppermute(behind, "z", ring(8, -1))
        pieces += [ahead, behind]
    pieces.append(lax.ppermute(ahead[:1], "z", ring(8, 1)))
    pieces.append(lax.ppermute(behind[1:], "z", ring(8, -1)))
    places = (0, 7, 1, 6, 2, 5, 3, 4, 4)
    which = ((0, 1),) * 7 + ((0,), (1,))

    normed, stats = pl.pallas_call(
        lambda *refs: normalise_kernel(feat_all, places, which, *refs),
        out_shape=(
            jax.ShapeDtypeStruct((17, rows + GAIN_ROWS, feat), BF16),
            jax.ShapeDtypeStruct((2, rows, 128), F32),
        ),
        in_specs=[VMEM] * (2 + len(pieces)),
        out_specs=(VMEM, VMEM),
        compiler_params=params(16),
        name="normalise",
    )(qk_gain, cotangent, *pieces)

    block = (rows + GAIN_ROWS, feat)

    def blocks(n):
        return jax.ShapeDtypeStruct((n,) + block, BF16)

    def cost(flops, nbytes):
        return pl.CostEstimate(flops=flops, bytes_accessed=nbytes, transcendentals=0)

    attended, ahead, behind, part_ahead, part_behind, grads, tail = pl.pallas_call(
        core_kernel,
        out_shape=(
            jax.ShapeDtypeStruct((rows, width), BF16),
            *(blocks(n) for n in (1, 1, 2, 2)),
            jax.ShapeDtypeStruct((rows, 3 * width), BF16),
            jax.ShapeDtypeStruct((GAIN_ROWS, rows), BF16),
        ),
        in_specs=[HBM] * 2,
        out_specs=(VMEM,) * 7,
        scratch_shapes=[
            pltpu.VMEM((2, 16) + weights.shape[2:], BF16),
            pltpu.VMEM(normed.shape, BF16),
            pltpu.VMEM((rows + GAIN_ROWS, 3 * width), F32),
            pltpu.SemaphoreType.DMA((17, 3)),
        ],
        compiler_params=params(50),
        name="core",
    )(normed, weights)
    *near, mine, other = pl.pallas_call(
        rest_kernel,
        out_shape=(*(blocks(2) for _ in range(4)),) + (jax.ShapeDtypeStruct(block, BF16),) * 2,
        in_specs=[VMEM] * 2 + [HBM],
        out_specs=(VMEM,) * 6,
        scratch_shapes=[
            pltpu.VMEM((5, 2, 2) + weights.shape[2:], BF16),
            pltpu.VMEM((2,) + block, BF16),
            pltpu.SemaphoreType.DMA((5, 2, 2)),
        ],
        compiler_params=params(50),
        cost_estimate=cost(2 * rows * 10 * feat * 3 * width, 6 * 2**20),
        name="rest",
    )(grads, tail, weights)

    def add(got, part, first, n_out, name):
        out = (blocks(2),) if n_out == 1 else (jax.ShapeDtypeStruct(block, BF16),) * 2
        return pl.pallas_call(
            lambda *refs: add_kernel(first, *refs),
            out_shape=out,
            in_specs=[VMEM] * 2,
            out_specs=(VMEM,) * n_out,
            compiler_params=params(16),
            cost_estimate=cost(10**6, 2**20),
            name=name,
        )(got, part)

    parts = [(part_ahead, part_behind), near[:2], near[2:]]
    for step in range(3):
        ahead = lax.ppermute(ahead, "z", ring(8, 1))
        behind = lax.ppermute(behind, "z", ring(8, -1))
        n_out = 2 if step == 2 else 1
        ahead, *ahead_other = add(ahead, parts[step][0], 0, n_out, "add_ahead")
        behind, *behind_other = add(behind, parts[step][1], 1 if step == 0 else 0, n_out, "add_behind")

    def across(step):
        return [(8 * k + i, 8 * (1 - k) + (i + step) % 8) for k in range(2) for i in range(8)]

    terms = (
        mine,
        lax.ppermute(other, "xl", ring(2, 1)),
        lax.ppermute(ahead, "z", ring(8, 1)),
        lax.ppermute(behind, "z", ring(8, -1)),
        lax.ppermute(ahead_other[0], ("xl", "z"), across(1)),
        lax.ppermute(behind_other[0], ("xl", "z"), across(-1)),
    )
    grad_tokens = pl.pallas_call(
        lambda *refs: final_kernel(feat_all, *refs),
        out_shape=jax.ShapeDtypeStruct((rows, feat), BF16),
        in_specs=[VMEM] * (3 + len(terms)),
        out_specs=VMEM,
        compiler_params=params(16),
        name="final_norm",
    )(tokens, gain, stats, *terms)
    return (attended, grad_tokens)


def solution(mesh):
    fine = Mesh(mesh.devices.reshape(2, 8, 2, 2, 8), ("xh", "y", "c", "xl", "z"))
    dp, mp = ("xh", "y", "c"), ("xl", "z")
    return jax.shard_map(
        per_device,
        mesh=fine,
        in_specs=(P(dp, mp), P(mp), P(None, dp, mp), P(), P(dp, mp)),
        out_specs=(P(dp, mp), P(dp, mp)),
        check_vma=False,
    )
```
